512 devices in a mesh: band: 16 (over z), fft: 32 (over x, y, core).
Axes of the slice: x: 4, y: 4, z: 16, core: 2. Of those that a mesh axis runs over, the one named last changes fastest.
Arguments:
- wave_coeffs: float32 [2, 16, 96, 4096], P(None, 'band', None, 'fft'), may hold values from -6 to 6
- correction: float32 [2, 16, 96, 4096], P(None, 'band', None, 'fft'), may hold values from -6 to 6
- kinetic: float32 [96, 4096], P(None, 'fft'), may hold values from 0.1 to 4
- z_slots: int32 [96, 4096], P(None, 'fft'), may hold values from 0 to 191, as said below
- stick_cols: int32 [2, 4096], replicated, may hold values from 0 to 191, as said below
- x_lines: int32 [96], replicated, may hold values from 0 to 191, as said below
- potential: float32 [192, 36864], P('fft'), may hold values from 0.5 to 3
Outputs:
- h_coeffs: float32 [2, 16, 96, 4096], P(None, 'band', None, 'fft')
- reduced: float32 [2, 16, 16], P(None, 'band')
The draws below stay inside these ranges and needn't reach their ends.
Inputs may be any that keep to these rules, and one draw needn't show every extreme that they name: `x_lines`: the 96 x frequencies are distinct. `stick_cols`: no two sticks share both their x line and their y frequency. `z_slots`: the 96 z frequencies of a stick are distinct.
All inputs are finite; a program needn't handle non-finite values.
Results may differ from the reference program's by a relative error of at most 0.000098.
Values sent between devices are 32-bit elements; how exact they have to be, the bound alone decides.
A program may use at most 128 MiB of HBM per device.

```python
import math
import jax
import jax.numpy as jnp
from jax import lax

GRID = 192
XSPAN = 96
SLOT = 96
STICKS = 4096
BANDS = 16


def distinct_pick(key, wanted, population):
    scores = jax.random.randint(key, (population,), 0, 65536) * population + jnp.arange(population, dtype=jnp.int32)
    scores = scores.at[0].set(-2).at[population - 1].set(-1)
    ranking = jnp.argsort(scores, stable=True)
    return ranking[:wanted].astype(jnp.int32)


def draw_x_lines(key, part):
    return distinct_pick(jax.random.fold_in(key, 11), XSPAN, GRID)


def draw_stick_cols(key, part):
    chosen = distinct_pick(jax.random.fold_in(key, 12), STICKS, XSPAN * GRID)
    return jnp.stack([chosen // GRID, chosen % GRID]).astype(jnp.int32)


def draw_z_slots(key, part):
    scores = jax.random.randint(jax.random.fold_in(key, 13), (STICKS, GRID), 0, 65536) * GRID + jnp.arange(GRID, dtype=jnp.int32)[None, :]
    scores = scores.at[0, 0].set(-2).at[0, GRID - 1].set(-1)
    ranking = jnp.argsort(scores, axis=1, stable=True)[:, :SLOT]
    return jnp.transpose(ranking).astype(jnp.int32)


def steps_of(own_key, dims, cuts, least, largest):
    def one(dim, shards_of):
        draws = jax.random.uniform(jax.random.fold_in(jax.random.fold_in(own_key, 6), dim), (shards_of,), jnp.float32, least / len(cuts), largest / len(cuts))
        return jnp.repeat(jnp.exp(draws), dims[dim] // shards_of).reshape((-1,) + (1,) * (len(dims) - dim - 1))

    gain = one(*cuts[0])
    for cut in cuts[1:]:
        gain = gain * one(*cut)
    return gain


def normal_values(key, dims, spread, bound, split=(), kind=jnp.bfloat16):
    entries = jax.random.normal(key, dims, jnp.float32) * spread
    if len(split) > 0:
        entries = steps_of(key, dims, split, -0.22, 0.18) * entries
    return jnp.clip(entries, min=-bound, max=bound).astype(kind)


def setup_inputs(seed: int = 0) -> dict:
    arg_keys = jax.random.split(jax.random.key(seed), 8)
    return {
        "wave_coeffs": normal_values(arg_keys[0], (2, BANDS, SLOT, STICKS), 1.0, 6.0, ((1, 16), (3, 32)), jnp.float32),
        "correction": normal_values(arg_keys[1], (2, BANDS, SLOT, STICKS), 1.0, 6.0, ((1, 16), (3, 32)), jnp.float32),
        "kinetic": jnp.clip(jnp.exp(math.log(4.0) - 3.6888794 * jax.random.uniform(arg_keys[2], (SLOT, STICKS), jnp.float32) ** steps_of(arg_keys[2], (SLOT, STICKS), ((1, 32),), -0.2, 0.2)), 0.1, 4.0),
        "z_slots": draw_z_slots(jax.random.fold_in(arg_keys[7], 71), 0),
        "stick_cols": draw_stick_cols(jax.random.fold_in(arg_keys[7], 71), 0),
        "x_lines": draw_x_lines(jax.random.fold_in(arg_keys[7], 71), 0),
        "potential": jnp.clip(0.5 + 2.5 * jax.random.uniform(arg_keys[6], (GRID, GRID * GRID), jnp.float32) ** steps_of(arg_keys[6], (GRID, GRID * GRID), ((0, 32),), -0.2, 0.2), 0.5, 3.0),
    }


def reference(wave_coeffs, correction, kinetic, z_slots, stick_cols, x_lines, potential):
    volume = float(GRID) ** 3
    x_freq = x_lines[stick_cols[0]]
    y_freq = stick_cols[1]
    potential_xyz = jnp.transpose(potential.reshape(GRID, GRID, GRID), (1, 2, 0))

    def one_band(band_pair):
        real_part, imag_part = band_pair
        empty = jnp.zeros((GRID, GRID, GRID), real_part.dtype)
        cube_real = empty.at[x_freq[None, :], y_freq[None, :], z_slots].set(real_part)
        cube_imag = empty.at[x_freq[None, :], y_freq[None, :], z_slots].set(imag_part)
        real_space = jnp.fft.ifftn(lax.complex(cube_real, cube_imag)) * volume
        returned = jnp.fft.fftn(real_space * potential_xyz) / volume
        picked = returned[x_freq[None, :], y_freq[None, :], z_slots]
        return (jnp.real(picked), jnp.imag(picked))
    v_real, v_imag = lax.map(one_band, (wave_coeffs[0], wave_coeffs[1]))
    h_real = kinetic * wave_coeffs[0] + v_real
    h_imag = kinetic * wave_coeffs[1] + v_imag
    h_coeffs = jnp.stack([h_real, h_imag])
    inverse_root = 1.0 / math.sqrt(STICKS * SLOT)

    def contract(left, right):
        return jnp.einsum('iks,jks->ij', left, right, precision=lax.Precision.HIGHEST)
    red_real = (contract(correction[0], h_real) + contract(correction[1], h_imag)) * inverse_root
    red_imag = (contract(correction[0], h_imag) - contract(correction[1], h_real)) * inverse_root
    return (h_coeffs, jnp.stack([red_real, red_imag]))
```

```python
import functools
import math

import jax
import jax.numpy as jnp
import numpy as np
from jax import lax
from jax.experimental import pallas as pl
from jax.experimental.pallas import tpu as pltpu
from jax.sharding import PartitionSpec as P

MESH = pl.DeviceIdType.MESH
F32 = jnp.float32
BF16 = jnp.bfloat16
G = 192
GP = 256
L = 96
K = 96
SL = 128
NF = 32
NB = 16
PL = 6
CP = 12
CPP = 16
NP = 16


def halves(table):
    hi = table.astype(jnp.bfloat16)
    lo = (table - hi.astype(np.float64)).astype(jnp.bfloat16)
    return hi, lo


def tables():
    f = np.arange(G)
    angle = 2.0 * math.pi * ((f[:, None] * f[None, :]) % G) / G
    cos, sin = np.cos(angle), np.sin(angle)
    plane_cos = np.zeros((GP, GP))
    plane_sin = np.zeros((GP, GP))
    plane_cos[:G, :G] = cos
    plane_sin[:G, :G] = sin
    forward = np.zeros((NF, CPP, 2, G))
    for part in range(2):
        rows = slice(part * PL, part * PL + PL)
        by_owner_cos = cos.reshape(NF, PL, G)
        by_owner_sin = sin.reshape(NF, PL, G)
        forward[:, rows, 0] = by_owner_sin if part else by_owner_cos
        forward[:, rows, 1] = by_owner_cos if part else -by_owner_sin
    forward = forward.reshape(NF * CPP, 2 * G)
    back = np.ascontiguousarray(forward.T)
    plane = np.stack(halves(plane_cos) + halves(plane_sin))
    return plane, np.stack(halves(forward)), np.stack(halves(back))


def split(value):
    hi = value.astype(BF16)
    lo = (value - hi.astype(F32)).astype(BF16)
    return hi, lo


def dot(a, b):
    return jnp.dot(a, b, preferred_element_type=F32)


def dot_nt(a, b):
    return lax.dot_general(a, b, (((1,), (1,)), ((), ())), preferred_element_type=F32)


def dot3(ah, al, bh, bl):
    return dot(ah, bh) + dot(al, bh) + dot(ah, bl)


def kernel(
    wave,
    corr,
    kinetic,
    zslots,
    sticks,
    xline,
    pot,
    plane_tab,
    fwd_tab,
    back_tab,
    h_out,
    red_out,
    send1,
    recv1,
    send2,
    recv2,
    dense,
    corr_all,
    potr,
    qt,
    pm,
    lhs_h,
    lhs_l,
    acc,
    s1h,
    s1l,
    s3h,
    s3l,
    o4h,
    o4l,
    back,
    ered,
    fsum,
    bsum,
    s1_send,
    s1_recv,
    s2_send,
    s2_recv,
    up_send,
    up_recv,
    dn_send,
    dn_recv,
    f_send,
    f_recv,
    b_send,
    b_recv,
):
    band = lax.axis_index("band")
    fft = lax.axis_index("fft")
    barrier = pltpu.get_barrier_semaphore()

    def to_fft(d):
        return {"fft": d}

    def to_band(d):
        return {"band": d}

    recv2[...] = jnp.zeros(recv2.shape, F32)

    def greet_fft(t, carry):
        d = lax.rem(fft + t, NF)
        pl.semaphore_signal(barrier, inc=1, device_id=to_fft(d), device_id_type=MESH)
        return carry

    def greet_band(t, carry):
        d = lax.rem(band + t, NB)
        pl.semaphore_signal(barrier, inc=1, device_id=to_band(d), device_id_type=MESH)
        return carry

    lax.fori_loop(1, NF, greet_fft, 0)
    lax.fori_loop(1, NB, greet_band, 0)

    corr_all[band] = corr[:, 0]

    def z_half(start):
        iota = lax.broadcasted_iota(jnp.int32, (G // 2, SL), 0) + start

        def step(k, carry):
            re, im = carry
            row = zslots[pl.ds(k, 1), :]
            hit = iota == row
            re = jnp.where(hit, wave[0, 0, pl.ds(k, 1), :], re)
            im = jnp.where(hit, wave[1, 0, pl.ds(k, 1), :], im)
            return re, im

        zero = jnp.zeros((G // 2, SL), F32)
        re, im = lax.fori_loop(0, K, step, (zero, zero), unroll=4)
        dense[pl.ds(start, G // 2), :] = re
        dense[pl.ds(G + start, G // 2), :] = im

    z_half(0)
    z_half(G // 2)
    dh, dl = split(dense[...])
    send1[...] = dot3(fwd_tab[0], fwd_tab[1], dh, dl).reshape(NF, CPP, SL)

    pl.semaphore_wait(barrier, NF - 1 + NB - 1)

    def copy1(dst, src):
        return pltpu.make_async_remote_copy(
            src_ref=send1.at[dst, pl.ds(0, CP)],
            dst_ref=recv1.at[src, pl.ds(0, CP)],
            send_sem=s1_send.at[dst],
            recv_sem=s1_recv.at[src],
            device_id=to_fft(dst),
            device_id_type=MESH,
        )

    def copy2(dst, src):
        return pltpu.make_async_remote_copy(
            src_ref=send2.at[dst, pl.ds(0, CP)],
            dst_ref=recv2.at[src, pl.ds(0, CP)],
            send_sem=s2_send.at[dst],
            recv_sem=s2_recv.at[src],
            device_id=to_fft(dst),
            device_id_type=MESH,
        )

    def send_one(t, carry):
        copy1(lax.rem(fft + t, NF), fft).start()
        return carry

    lax.fori_loop(1, NF, send_one, 0)
    recv1[fft] = send1[fft]

    above = lax.rem(band + 1, NB)
    below = lax.rem(band + NB - 1, NB)

    def up_copy(t):
        slot = lax.rem(band - t + 1 + NB, NB)
        return pltpu.make_async_remote_copy(
            src_ref=corr_all.at[slot],
            dst_ref=corr_all.at[slot],
            send_sem=up_send.at[t - 1],
            recv_sem=up_recv.at[t - 1],
            device_id=to_band(above),
            device_id_type=MESH,
        )

    def down_copy(t):
        slot = lax.rem(band + t - 1, NB)
        return pltpu.make_async_remote_copy(
            src_ref=corr_all.at[slot],
            dst_ref=corr_all.at[slot],
            send_sem=dn_send.at[t - 1],
            recv_sem=dn_recv.at[t - 1],
            device_id=to_band(below),
            device_id_type=MESH,
        )

    def ring(t):
        if t > 1:
            up_copy(t - 1).wait_recv()
        if t <= 8:
            up_copy(t).start()
        if 1 < t <= 8:
            down_copy(t - 1).wait_recv()
        if t <= 7:
            down_copy(t).start()

    ring(1)

    y_iota = lax.broadcasted_iota(jnp.int32, (GP, GP), 0)
    l_iota = lax.broadcasted_iota(jnp.int32, (L, GP), 0)

    def one_hots(t, carry):
        lane = pl.ds(pl.multiple_of(t * GP, GP), GP)
        hit = y_iota == sticks[1:2, lane]
        qt[t] = jnp.where(hit, 1.0, 0.0).astype(BF16)
        line = l_iota == sticks[0:1, lane]
        pm[t] = jnp.where(line, 1.0, 0.0).astype(BF16)
        return carry

    lax.fori_loop(0, NP, one_hots, 0)

    potr[...] = jnp.zeros(potr.shape, F32)

    def relay(q, carry):
        block = pot[:, pl.ds(pl.multiple_of(q * 2 * G, SL), 2 * G)]
        even = block[:, :G]
        odd = block[:, G:]
        for p in range(PL):
            potr[p, pl.ds(2 * q, 1), 0:G] = even[p : p + 1]
            potr[p, pl.ds(2 * q + 1, 1), 0:G] = odd[p : p + 1]
        return carry

    lax.fori_loop(0, G // 2, relay, 0)

    ered[...] = jnp.zeros(ered.shape, F32)
    ered[:, 0:L] = jnp.where(
        lax.broadcasted_iota(jnp.int32, (GP, L), 0) == xline[...], 1.0, 0.0
    )
    pick = ered[...]
    pick_b = pick.astype(BF16)
    pick_t = jnp.transpose(pick)[:L].astype(BF16)
    ch, cl, sh, sl = plane_tab[0], plane_tab[1], plane_tab[2], plane_tab[3]

    def x_tables(c, s):
        xc = dot(c[:G], pick_b).astype(BF16)
        xs = dot(s[:G], pick_b).astype(BF16)
        forward = jnp.concatenate(
            [
                jnp.concatenate([xc, -xs], axis=1),
                jnp.concatenate([xs, xc], axis=1),
            ],
            axis=0,
        )
        yc = dot(pick_t, c)[:, :G].astype(BF16)
        ys = dot(pick_t, s)[:, :G].astype(BF16)
        back_re = jnp.concatenate([yc, -ys], axis=0)
        back_im = jnp.concatenate([ys, yc], axis=0)
        return forward, back_re, back_im

    xf_h, xr_h, xi_h = x_tables(ch, sh)
    xf_l, xr_l, xi_l = x_tables(cl, sl)

    acc[...] = jnp.zeros(acc.shape, F32)
    my_pair = fft // 2

    def scatter_step(t, carry):
        pair = lax.rem(my_pair + t, NP)
        a = 2 * pair
        b = a + 1

        @pl.when(a != fft)
        def _():
            copy1(a, a).wait_recv()

        @pl.when(b != fft)
        def _():
            copy1(b, b).wait_recv()

        x = jnp.concatenate([recv1[a], recv1[b]], axis=1)
        mask = pm[pair]
        for cp in range(CP):
            row = jnp.broadcast_to(x[cp : cp + 1], (16, GP))
            hi, lo = split(row)
            lhs_h[cp * L : cp * L + L] = (mask.reshape(L // 16, 16, GP) * hi[None]).reshape(L, GP)
            lhs_l[cp * L : cp * L + L] = (mask.reshape(L // 16, 16, GP) * lo[None]).reshape(L, GP)
        q = qt[pair]
        acc[...] += dot_nt(lhs_h[...], q) + dot_nt(lhs_l[...], q)
        return carry

    lax.fori_loop(0, 6, scatter_step, 0)
    ring(2)
    lax.fori_loop(6, NP, scatter_step, 0)
    ring(3)

    s1h[...] = jnp.zeros(s1h.shape, BF16)
    s1l[...] = jnp.zeros(s1l.shape, BF16)
    half = PL * L

    def y_forward(p, carry):
        re_h, re_l = split(acc[pl.ds(p * L, L), :])
        im_h, im_l = split(acc[pl.ds(half + p * L, L), :])
        ah = jnp.concatenate([re_h, im_h], axis=0)
        al = jnp.concatenate([re_l, im_l], axis=0)
        u = dot3(ah, al, ch, cl)
        v = dot3(ah, al, sh, sl)
        hi, lo = split(u[:L] - v[L:])
        s1h[p, 0:L] = hi
        s1l[p, 0:L] = lo
        hi, lo = split(v[:L] + u[L:])
        s1h[p, SL : SL + L] = hi
        s1l[p, SL : SL + L] = lo
        return carry

    lax.fori_loop(0, PL, y_forward, 0)
    ring(4)

    def x_both(p, carry):
        r = dot3(xf_h, xf_l, s1h[p], s1l[p])
        v = potr[p]
        re_h, re_l = split(r[:G] * v)
        im_h, im_l = split(r[G:] * v)
        s = dot3(xr_h, xr_l, re_h, re_l) + dot3(xi_h, xi_l, im_h, im_l)
        hi, lo = split(s)
        s3h[p] = hi
        s3l[p] = lo
        return carry

    lax.fori_loop(0, 3, x_both, 0)
    ring(5)
    lax.fori_loop(3, PL, x_both, 0)
    ring(6)

    def y_back(p, carry):
        ah, al = s3h[p], s3l[p]
        u = dot3(ah, al, ch, cl)
        v = dot3(ah, al, sh, sl)
        hi, lo = split(u[:L] + v[L:])
        o4h[pl.ds(p * L, L), :] = hi
        o4l[pl.ds(p * L, L), :] = lo
        hi, lo = split(u[L:] - v[:L])
        o4h[pl.ds(half + p * L, L), :] = hi
        o4l[pl.ds(half + p * L, L), :] = lo
        return carry

    lax.fori_loop(0, PL, y_back, 0)
    ring(7)

    def gather_step(t, carry):
        pair = lax.rem(my_pair + t, NP)
        a = 2 * pair
        b = a + 1
        q = qt[pair]
        lane = pl.ds(pl.multiple_of(pair * GP, GP), GP)
        line = l_iota == sticks[0:1, lane]
        full = dot(o4h[...], q) + dot(o4l[...], q)
        for cp in range(CP):
            v = jnp.sum(jnp.where(line, full[cp * L : cp * L + L], 0.0), axis=0, keepdims=True)
            send2[a, cp : cp + 1, :] = v[:, :SL]
            send2[b, cp : cp + 1, :] = v[:, SL:]

        @pl.when(a != fft)
        def _():
            copy2(a, fft).start()

        @pl.when(b != fft)
        def _():
            copy2(b, fft).start()

        return carry

    lax.fori_loop(1, 8, gather_step, 0)
    ring(8)
    lax.fori_loop(8, NP + 1, gather_step, 0)
    recv2[fft, 0:CP] = send2[fft, 0:CP]
    ring(9)

    def wait_two(t, carry):
        src = lax.rem(fft + t, NF)
        copy2(src, src).wait_recv()
        return carry

    lax.fori_loop(1, NF, wait_two, 0)

    bh, bl = split(recv2[...].reshape(NF * CPP, SL))
    back[...] = dot3(back_tab[0], back_tab[1], bh, bl)
    zs = zslots[...]

    def pick_step(z, carry):
        re, im = carry
        hit = zs == z
        re = jnp.where(hit, back[pl.ds(z, 1), :], re)
        im = jnp.where(hit, back[pl.ds(G + z, 1), :], im)
        return re, im

    zero = jnp.zeros((K, SL), F32)
    v_re, v_im = lax.fori_loop(0, G, pick_step, (zero, zero), unroll=4)
    scale = 1.0 / float(G) ** 3
    kin = kinetic[...]
    h_re = kin * wave[0, 0] + v_re * scale
    h_im = kin * wave[1, 0] + v_im * scale
    h_out[0, 0] = h_re
    h_out[1, 0] = h_im

    row_iota = lax.broadcasted_iota(jnp.int32, (2 * NB, SL), 0)

    def contract(i, total):
        c_re = corr_all[i, 0]
        c_im = corr_all[i, 1]
        re = jnp.sum(c_re * h_re + c_im * h_im, axis=0, keepdims=True)
        im = jnp.sum(c_re * h_im - c_im * h_re, axis=0, keepdims=True)
        total = jnp.where(row_iota == i, re, total)
        return jnp.where(row_iota == NB + i, im, total)

    total = lax.fori_loop(0, NB, contract, jnp.zeros((2 * NB, SL), F32))
    column = jnp.sum(total, axis=1, keepdims=True)
    lane_iota = lax.broadcasted_iota(jnp.int32, (2 * NB, SL), 1)
    mine = jnp.sum(jnp.where(row_iota == lane_iota, column, 0.0), axis=0, keepdims=True)
    fsum[fft] = mine

    def f_copy(dst, src):
        return pltpu.make_async_remote_copy(
            src_ref=fsum.at[src],
            dst_ref=fsum.at[src],
            send_sem=f_send.at[dst],
            recv_sem=f_recv.at[src],
            device_id=to_fft(dst),
            device_id_type=MESH,
        )

    def b_copy(dst, src):
        return pltpu.make_async_remote_copy(
            src_ref=bsum.at[src],
            dst_ref=bsum.at[src],
            send_sem=b_send.at[dst],
            recv_sem=b_recv.at[src],
            device_id=to_band(dst),
            device_id_type=MESH,
        )

    def f_start(t, carry):
        f_copy(lax.rem(fft + t, NF), fft).start()
        return carry

    def f_wait(t, carry):
        src = lax.rem(fft + t, NF)
        f_copy(src, src).wait_recv()
        return carry

    lax.fori_loop(1, NF, f_start, 0)
    lax.fori_loop(1, NF, f_wait, 0)
    bsum[band] = jnp.sum(fsum[...], axis=0)

    def b_start(t, carry):
        b_copy(lax.rem(band + t, NB), band).start()
        return carry

    def b_wait(t, carry):
        src = lax.rem(band + t, NB)
        b_copy(src, src).wait_recv()
        return carry

    lax.fori_loop(1, NB, b_start, 0)
    lax.fori_loop(1, NB, b_wait, 0)

    block = bsum[...].reshape(NB, SL)
    root = 1.0 / math.sqrt(NF * SL * K)
    b_row = lax.broadcasted_iota(jnp.int32, (NB, SL), 0)
    b_lane = lax.broadcasted_iota(jnp.int32, (NB, SL), 1)
    for part in range(2):
        column = jnp.sum(
            jnp.where(b_lane == part * NB + band, block, 0.0), axis=1, keepdims=True
        )
        line = jnp.sum(jnp.where(b_row == b_lane, column, 0.0), axis=0, keepdims=True)
        red_out[part] = line[:, :NB] * root

    def drain(t, carry):
        d = lax.rem(fft + t, NF)
        copy1(d, fft).wait_send()
        copy2(d, fft).wait_send()
        f_copy(d, fft).wait_send()
        return carry

    lax.fori_loop(1, NF, drain, 0)

    def drain_band(t, carry):
        b_copy(lax.rem(band + t, NB), band).wait_send()
        return carry

    lax.fori_loop(1, NB, drain_band, 0)
    for t in range(1, 9):
        up_copy(t).wait_send()
        if t <= 7:
            down_copy(t).wait_send()


def local(wave, corr, kinetic, zslots, sticks, xlines, pot):
    plane, forward, back = tables()
    dma = pltpu.SemaphoreType.DMA
    vmem = pltpu.VMEM
    return pl.pallas_call(
        kernel,
        out_shape=(
            jax.ShapeDtypeStruct((2, 1, K, SL), F32),
            jax.ShapeDtypeStruct((2, 1, NB), F32),
        ),
        in_specs=[pl.BlockSpec(memory_space=vmem)] * 10,
        out_specs=(pl.BlockSpec(memory_space=vmem),) * 2,
        scratch_shapes=[
            vmem((NF, CPP, SL), F32),
            vmem((NF, CPP, SL), F32),
            vmem((NF, CPP, SL), F32),
            vmem((NF, CPP, SL), F32),
            vmem((2 * G, SL), F32),
            vmem((NB, 2, K, SL), F32),
            vmem((PL, G, GP), F32),
            vmem((NP, GP, GP), BF16),
            vmem((NP, L, GP), BF16),
            vmem((CP * L, GP), BF16),
            vmem((CP * L, GP), BF16),
            vmem((CP * L, GP), F32),
            vmem((PL, GP, GP), BF16),
            vmem((PL, GP, GP), BF16),
            vmem((PL, 2 * L, GP), BF16),
            vmem((PL, 2 * L, GP), BF16),
            vmem((CP * L, GP), BF16),
            vmem((CP * L, GP), BF16),
            vmem((2 * G, SL), F32),
            vmem((GP, SL), F32),
            vmem((NF, 1, SL), F32),
            vmem((NB, 1, SL), F32),
            dma((NF,)),
            dma((NF,)),
            dma((NF,)),
            dma((NF,)),
            dma((8,)),
            dma((8,)),
            dma((8,)),
            dma((8,)),
            dma((NF,)),
            dma((NF,)),
            dma((NB,)),
            dma((NB,)),
        ],
        compiler_params=pltpu.CompilerParams(
            collective_id=0,
            has_side_effects=True,
            vmem_limit_bytes=48 * 1024 * 1024,
        ),
    )(
        wave,
        corr,
        kinetic,
        zslots,
        sticks,
        xlines.reshape(1, L),
        pot,
        jnp.asarray(plane),
        jnp.asarray(forward),
        jnp.asarray(back),
    )


def solution(mesh):
    return jax.shard_map(
        local,
        mesh=mesh,
        in_specs=(
            P(None, "band", None, "fft"),
            P(None, "band", None, "fft"),
            P(None, "fft"),
            P(None, "fft"),
            P(),
            P(),
            P("fft", None),
        ),
        out_specs=(P(None, "band", None, "fft"), P(None, "band", None)),
        check_vma=False,
    )
```

```python
import functools
import math

import jax
import jax.numpy as jnp
import numpy as np
from jax import lax
from jax.experimental import pallas as pl
from jax.experimental.pallas import tpu as pltpu
from jax.sharding import PartitionSpec as P

MESH = pl.DeviceIdType.MESH
F32 = jnp.float32
BF16 = jnp.bfloat16
G = 192
GP = 256
L = 96
K = 96
SL = 128
NF = 32
NB = 16
PL = 6
CP = 12
CPP = 16
NC = 4
CS = 1024
CD = 8
A = 72
Q = 24


def halves(table):
    hi = table.astype(jnp.bfloat16)
    lo = (table - hi.astype(np.float64)).astype(jnp.bfloat16)
    return hi, lo


def three_beside(table):
    hi, lo = halves(table)
    return np.concatenate([hi, lo, hi], axis=1)


def three_below(table):
    hi, lo = halves(table)
    return np.concatenate([hi, hi, lo], axis=0)


def tables():
    f = np.arange(G)
    angle = 2.0 * math.pi * ((f[:, None] * f[None, :]) % G) / G
    cos, sin = np.cos(angle), np.sin(angle)
    plane_cos = np.zeros((GP, GP))
    plane_sin = np.zeros((GP, GP))
    plane_cos[:G, :G] = cos
    plane_sin[:G, :G] = sin
    forward = np.zeros((NF, CPP, 2, G))
    for part in range(2):
        rows = slice(part * PL, part * PL + PL)
        by_owner_cos = cos.reshape(NF, PL, G)
        by_owner_sin = sin.reshape(NF, PL, G)
        forward[:, rows, 0] = by_owner_sin if part else by_owner_cos
        forward[:, rows, 1] = by_owner_cos if part else -by_owner_sin
    forward = forward.reshape(NF * CPP, 2 * G)
    back = np.ascontiguousarray(forward.T)
    plane = three_below(np.concatenate([plane_cos, plane_sin], axis=1))
    order = np.concatenate([f[0::2], f[1::2]])
    lines = np.concatenate([plane_cos[order], plane_sin[order], plane_cos[order]], axis=0)
    return plane, np.stack(halves(lines)), three_beside(forward), three_beside(back)


def split(value):
    hi = value.astype(BF16)
    lo = (value - hi.astype(F32)).astype(BF16)
    return hi, lo


def dot(a, b):
    return jnp.dot(a, b, preferred_element_type=F32)


def dot_nt(a, b):
    return lax.dot_general(a, b, (((1,), (1,)), ((), ())), preferred_element_type=F32)


def abreast(value):
    hi, lo = split(value)
    return jnp.concatenate([hi, lo, hi], axis=1)


def stacked(value):
    hi, lo = split(value)
    return jnp.concatenate([hi, hi, lo], axis=0)


def kernel(
    wave_in,
    corr_in,
    kinetic_in,
    zslots_in,
    sticks_in,
    xline_in,
    pot_in,
    plane_in,
    x_in,
    fwd_in,
    back_in,
    h_out,
    red_out,
    wave,
    kinetic,
    zslots,
    sticks,
    xline,
    pot,
    plane_tab,
    x_tab,
    fwd_tab,
    back_tab,
    in_sem,
    send1,
    recv1,
    send2,
    recv2,
    dense,
    corr_all,
    potr,
    qt,
    rows,
    lhs,
    acc,
    s1,
    xf,
    xb,
    s3,
    ob,
    o4,
    back,
    fsum,
    bsum,
    s1_send,
    s1_recv,
    s2_send,
    s2_recv,
    up_send,
    up_recv,
    dn_send,
    dn_recv,
    f_send,
    f_recv,
    b_send,
    b_recv,
):
    band = lax.axis_index("band")
    fft = lax.axis_index("fft")
    barrier = pltpu.get_barrier_semaphore()

    def to_fft(d):
        return {"fft": d}

    def to_band(d):
        return {"band": d}

    loads = [
        pltpu.make_async_copy(src, dst, in_sem.at[n])
        for n, (src, dst) in enumerate(
            (
                (zslots_in, zslots),
                (wave_in, wave),
                (fwd_in, fwd_tab),
                (corr_in.at[:, 0], corr_all.at[band]),
                (sticks_in, sticks),
                (pot_in, pot.at[pl.ds(0, PL)]),
                (xline_in, xline),
                (plane_in, plane_tab),
                (x_in, x_tab),
                (kinetic_in, kinetic),
                (back_in, back_tab),
            )
        )
    ]
    for load in loads:
        load.start()

    recv2[...] = jnp.zeros(recv2.shape, F32)

    def greet_fft(t, carry):
        d = lax.rem(fft + t, NF)
        pl.semaphore_signal(barrier, inc=1, device_id=to_fft(d), device_id_type=MESH)
        return carry

    def greet_band(t, carry):
        d = lax.rem(band + t, NB)
        pl.semaphore_signal(barrier, inc=1, device_id=to_band(d), device_id_type=MESH)
        return carry

    lax.fori_loop(1, NF, greet_fft, 0)
    lax.fori_loop(1, NB, greet_band, 0)

    loads[0].wait()
    loads[1].wait()

    def z_half(start):
        iota = lax.broadcasted_iota(jnp.int32, (G // 2, SL), 0) + start

        def step(k, carry):
            re, im = carry
            row = zslots[pl.ds(k, 1), :]
            hit = iota == row
            re = jnp.where(hit, wave[0, 0, pl.ds(k, 1), :], re)
            im = jnp.where(hit, wave[1, 0, pl.ds(k, 1), :], im)
            return re, im

        zero = jnp.zeros((G // 2, SL), F32)
        re, im = lax.fori_loop(0, K, step, (zero, zero), unroll=4)
        dense[pl.ds(start, G // 2), :] = re
        dense[pl.ds(G + start, G // 2), :] = im

    z_half(0)
    z_half(G // 2)
    loads[2].wait()
    send1[...] = dot(fwd_tab[...], stacked(dense[...])).reshape(NF, CPP, SL)

    pl.semaphore_wait(barrier, NF - 1 + NB - 1)

    def copy1(dst, src):
        return pltpu.make_async_remote_copy(
            src_ref=send1.at[dst, pl.ds(0, CP)],
            dst_ref=recv1.at[src, pl.ds(0, CP)],
            send_sem=s1_send.at[dst],
            recv_sem=s1_recv.at[src],
            device_id=to_fft(dst),
            device_id_type=MESH,
        )

    def copy2(dst, src):
        return pltpu.make_async_remote_copy(
            src_ref=send2.at[dst, pl.ds(0, CP)],
            dst_ref=recv2.at[src, pl.ds(0, CP)],
            send_sem=s2_send.at[dst],
            recv_sem=s2_recv.at[src],
            device_id=to_fft(dst),
            device_id_type=MESH,
        )

    def send_one(t, carry):
        copy1(lax.rem(fft + t, NF), fft).start()
        return carry

    lax.fori_loop(1, NF, send_one, 0)
    recv1[fft] = send1[fft]

    above = lax.rem(band + 1, NB)
    below = lax.rem(band + NB - 1, NB)

    def ring_copy(up, t, part):
        slot = lax.rem(band + NB + 1 - t, NB) if up else lax.rem(band + t - 1, NB)
        return pltpu.make_async_remote_copy(
            src_ref=corr_all.at[slot, part],
            dst_ref=corr_all.at[slot, part],
            send_sem=(up_send if up else dn_send).at[t - 1, part],
            recv_sem=(up_recv if up else dn_recv).at[t - 1, part],
            device_id=to_band(above if up else below),
            device_id_type=MESH,
        )

    def ring(t, part):
        for up in (True, False):
            last = 8 if up == (part == 0) else 7
            if isinstance(t, int):
                if 1 < t <= last + 1:
                    ring_copy(up, t - 1, part).wait_recv()
                if t <= last:
                    ring_copy(up, t, part).start()
            else:
                ring_copy(up, t - 1, part).wait_recv()
                ring_copy(up, t, part).start()

    loads[3].wait()
    ring(1, 0)
    ring(1, 1)
    for load in loads[4:]:
        load.wait()

    def hot(condition):
        return jnp.where(condition, 1.0, 0.0).astype(BF16)

    cell_iota = lax.broadcasted_iota(jnp.int32, (GP, CS), 0)
    for n in range(NC):
        span = slice(n * CS, n * CS + CS)
        line = sticks[0:1, span]
        y = sticks[1:2, span]
        top = y < SL
        rows[n] = jnp.where(top, line >> 1, 2 * Q + (line >> 2))
        lane = jnp.where(top, (line & 1) * SL + y, (line & 3) * (SL // 2) + y - SL)
        qt[n] = hot(cell_iota == lane)

    def relay(q, carry):
        for j in range(3):
            potr[j, pl.ds(pl.multiple_of(q * 8, 8), 8), :] = pot[
                :, pl.ds(pl.multiple_of((q * 3 + j) * SL, SL), SL)
            ]
        return carry

    lax.fori_loop(0, G // 2, relay, 0, unroll=4)

    spot = lax.broadcasted_iota(jnp.int32, (L, GP), 1)
    kind = jnp.where(spot >= Q, 1, 0) + jnp.where(spot >= 2 * Q, 1, 0) + jnp.where(spot >= 3 * Q, 1, 0)
    order = hot(lax.broadcasted_iota(jnp.int32, (L, GP), 0) == 4 * (spot - Q * kind) + kind)
    pick = dot(hot(lax.broadcasted_iota(jnp.int32, (GP, L), 0) == xline[...]), order)
    pick_a = pick[:, :SL].astype(BF16)
    pick_t = jnp.transpose(pick[:, :SL])[:L].astype(BF16)
    first = lax.broadcasted_iota(jnp.int32, (L, 2 * G), 1) < G
    for n in range(2):
        xc = dot(x_tab[n, 0:G], pick_a).astype(BF16)
        xs = dot(x_tab[n, G : 2 * G], pick_a).astype(BF16)
        re = jnp.concatenate([xc, -xs], axis=1)
        im = jnp.concatenate([xs, xc], axis=1)
        yr = dot_nt(pick_t, x_tab[n, 0 : 2 * G]).astype(BF16)
        yi = dot_nt(pick_t, x_tab[n, G : 3 * G])
        yi = jnp.where(first, -yi, yi).astype(BF16)
        for k in (0, 2) if n == 0 else (1,):
            xf[0:G, k * GP : k * GP + GP] = re
            xf[G:, k * GP : k * GP + GP] = im
            xb[0:L, k * 2 * G : (k + 1) * 2 * G] = yr
            xb[L:, k * 2 * G : (k + 1) * 2 * G] = yi

    my_chunk = fft // CD
    a_iota = lax.broadcasted_iota(jnp.int32, (A, GP), 0)
    for n in range(NC):
        chunk = lax.rem(my_chunk + n, NC)

        def arrive(t, carry):
            src = chunk * CD + t

            @pl.when(src != fft)
            def _():
                copy1(src, src).wait_recv()

            return carry

        lax.fori_loop(0, CD, arrive, 0)
        for i in range(CD // 2):
            src = chunk * CD + 2 * i
            x = jnp.concatenate([recv1[src], recv1[src + 1]], axis=1)
            hi, lo = split(x)
            hi = hi.astype(F32)
            lo = lo.astype(F32)
            here = a_iota == rows[chunk][:, i * GP : i * GP + GP]
            for cp in range(0, CP, 2):
                at = slice(cp * A, cp * A + 2 * A)
                for j, v in enumerate((hi, lo)):
                    two = [jnp.where(here, v[cp + k : cp + k + 1], 0.0) for k in range(2)]
                    k = (j * CD // 2 + i) * GP
                    lhs[n % 2, at, k : k + GP] = jnp.concatenate(two, axis=0).astype(BF16)
        q = qt[chunk]
        cells = dot_nt(lhs[n % 2], jnp.concatenate([q, q], axis=1))
        for h in range(2):
            half = cells[:, h * SL : h * SL + SL]
            if n == 0:
                acc[h] = half
            else:
                acc[h] += half
        ring(2 + n // 2, n % 2)

    def line_block(cp):
        blocks = []
        for m in range(4):
            top = acc[m % 2, pl.ds(cp * A + m // 2, Q, stride=2), :]
            low = acc[m // 2, cp * A + 2 * Q : cp * A + A, :]
            if m % 2:
                low = pltpu.roll(low, SL // 2, 1)
            blocks.append(jnp.concatenate([top, low], axis=1))
        return jnp.concatenate(blocks, axis=0)

    third = 3 * L
    for k in range(6):
        s1[:, k * SL + L : k * SL + SL] = jnp.zeros((2, SL - L, 3 * GP), BF16)
    for n in range(2):
        planes = range(3 * n, 3 * n + 3)
        a = jnp.concatenate([line_block(c * PL + p) for c in range(2) for p in planes], axis=0)
        uv = dot(abreast(a), plane_tab[...])
        u, v = uv[:, :GP], uv[:, GP:]
        re = split(u[:third] - v[third:])
        im = split(v[:third] + u[third:])
        for i in range(3):
            at = slice(i * L, i * L + L)
            for k in range(3):
                s1[n, k * GP : k * GP + L, i * GP : i * GP + GP] = re[k // 2][at]
                s1[n, k * GP + SL : k * GP + SL + L, i * GP : i * GP + GP] = im[k // 2][at]
        ring(4, n)

    for n in range(2):
        r = dot(xf[...], s1[n])
        parts = []
        for i in range(3):
            v = [potr[j, pl.ds(3 * n + i, G // 2, stride=8), :] for j in range(3)]
            w = pltpu.roll(jnp.concatenate(v, axis=1), G, 1)
            v = jnp.concatenate([jnp.concatenate(v[:2], axis=1), w[:, :GP]], axis=0)
            parts.append(r[:, i * GP : i * GP + GP] * jnp.concatenate([v, v], axis=0))
        s3[n] = dot(xb[...], stacked(jnp.concatenate(parts, axis=1)))
        ring(5 + n, 0)
        ring(5 + n, 1)

    low_lane = lax.broadcasted_iota(jnp.int32, (Q, SL), 1) < SL // 2
    for n in range(2):
        a = jnp.concatenate([s3[n, :, i * GP : i * GP + GP] for i in range(3)], axis=0)
        uv = dot(abreast(a), plane_tab[...])
        u, v = uv[:, :GP], uv[:, GP:]
        for i in range(3):
            top = slice(2 * i * L, 2 * i * L + L)
            low = slice(2 * i * L + L, 2 * i * L + 2 * L)
            for c, lines in enumerate((u[top] + v[low], u[low] - v[top])):
                cp = c * PL + 3 * n + i
                block = [lines[m * Q : m * Q + Q] for m in range(4)]
                for m in range(4):
                    ob[m % 2, pl.ds(cp * A + m // 2, Q, stride=2), :] = block[m][:, :SL]
                for h in range(2):
                    ob[h, cp * A + 2 * Q : cp * A + A, :] = jnp.where(
                        low_lane,
                        block[2 * h][:, SL:],
                        pltpu.roll(block[2 * h + 1][:, SL:], SL // 2, 1),
                    )
        ring(7, n)
    hi, lo = split(jnp.concatenate([ob[0], ob[1]], axis=1))
    o4[:, :GP] = hi
    o4[:, GP:] = lo

    def gather_step(n, carry):
        chunk = lax.rem(my_chunk + n, NC)
        for i in range(CD // 2):
            span = slice(i * GP, i * GP + GP)
            q = qt[chunk, :, span]
            here = a_iota == rows[chunk][:, span]
            full = dot(o4[...], jnp.concatenate([q, q], axis=0))
            for cp in range(CP):
                v = jnp.where(here, full[cp * A : cp * A + A], 0.0)
                v = jnp.sum(v, axis=0, keepdims=True)
                send2[chunk * CD + 2 * i, cp : cp + 1, :] = v[:, :SL]
                send2[chunk * CD + 2 * i + 1, cp : cp + 1, :] = v[:, SL:]

        def leave(t, inner):
            dst = chunk * CD + t

            @pl.when(dst != fft)
            def _():
                copy2(dst, fft).start()

            return inner

        return lax.fori_loop(0, CD, leave, carry)

    lax.fori_loop(1, 3, gather_step, 0)
    ring(8, 0)
    lax.fori_loop(3, NC + 1, gather_step, 0)
    ring(8, 1)
    recv2[fft, 0:CP] = send2[fft, 0:CP]

    def wait_two(t, carry):
        src = lax.rem(fft + t, NF)
        copy2(src, src).wait_recv()
        return carry

    lax.fori_loop(1, NF, wait_two, 0)

    back[...] = dot(back_tab[...], stacked(recv2[...].reshape(NF * CPP, SL)))
    zs = zslots[...]

    def pick_step(z, carry):
        re, im = carry
        hit = zs == z
        re = jnp.where(hit, back[pl.ds(z, 1), :], re)
        im = jnp.where(hit, back[pl.ds(G + z, 1), :], im)
        return re, im

    zero = jnp.zeros((K, SL), F32)
    v_re, v_im = lax.fori_loop(0, G, pick_step, (zero, zero), unroll=4)
    scale = 1.0 / float(G) ** 3
    kin = kinetic[...]
    h_re = kin * wave[0, 0] + v_re * scale
    h_im = kin * wave[1, 0] + v_im * scale
    h_out[0, 0] = h_re
    h_out[1, 0] = h_im

    ring(9, 0)
    ring(9, 1)
    row_iota = lax.broadcasted_iota(jnp.int32, (2 * NB, SL), 0)

    def contract(i, total):
        c_re = corr_all[i, 0]
        c_im = corr_all[i, 1]
        re = jnp.sum(c_re * h_re + c_im * h_im, axis=0, keepdims=True)
        im = jnp.sum(c_re * h_im - c_im * h_re, axis=0, keepdims=True)
        total = jnp.where(row_iota == i, re, total)
        return jnp.where(row_iota == NB + i, im, total)

    total = lax.fori_loop(0, NB, contract, jnp.zeros((2 * NB, SL), F32))
    column = jnp.sum(total, axis=1, keepdims=True)
    lane_iota = lax.broadcasted_iota(jnp.int32, (2 * NB, SL), 1)
    mine = jnp.sum(jnp.where(row_iota == lane_iota, column, 0.0), axis=0, keepdims=True)
    fsum[fft] = mine

    def f_copy(dst, src):
        return pltpu.make_async_remote_copy(
            src_ref=fsum.at[src],
            dst_ref=fsum.at[src],
            send_sem=f_send.at[dst],
            recv_sem=f_recv.at[src],
            device_id=to_fft(dst),
            device_id_type=MESH,
        )

    def b_copy(dst, src):
        return pltpu.make_async_remote_copy(
            src_ref=bsum.at[src],
            dst_ref=bsum.at[src],
            send_sem=b_send.at[dst],
            recv_sem=b_recv.at[src],
            device_id=to_band(dst),
            device_id_type=MESH,
        )

    def f_start(t, carry):
        f_copy(lax.rem(fft + t, NF), fft).start()
        return carry

    def f_wait(t, carry):
        src = lax.rem(fft + t, NF)
        f_copy(src, src).wait_recv()
        return carry

    lax.fori_loop(1, NF, f_start, 0)
    lax.fori_loop(1, NF, f_wait, 0)
    bsum[band] = jnp.sum(fsum[...], axis=0)

    def b_start(t, carry):
        b_copy(lax.rem(band + t, NB), band).start()
        return carry

    def b_wait(t, carry):
        src = lax.rem(band + t, NB)
        b_copy(src, src).wait_recv()
        return carry

    lax.fori_loop(1, NB, b_start, 0)
    lax.fori_loop(1, NB, b_wait, 0)

    block = bsum[...].reshape(NB, SL)
    root = 1.0 / math.sqrt(NF * SL * K)
    b_row = lax.broadcasted_iota(jnp.int32, (NB, SL), 0)
    b_lane = lax.broadcasted_iota(jnp.int32, (NB, SL), 1)
    for part in range(2):
        column = jnp.sum(
            jnp.where(b_lane == part * NB + band, block, 0.0), axis=1, keepdims=True
        )
        line = jnp.sum(jnp.where(b_row == b_lane, column, 0.0), axis=0, keepdims=True)
        red_out[part] = line[:, :NB] * root

    def drain(t, carry):
        d = lax.rem(fft + t, NF)
        copy1(d, fft).wait_send()
        copy2(d, fft).wait_send()
        f_copy(d, fft).wait_send()
        return carry

    lax.fori_loop(1, NF, drain, 0)

    def drain_band(t, carry):
        b_copy(lax.rem(band + t, NB), band).wait_send()
        return carry

    lax.fori_loop(1, NB, drain_band, 0)
    for part in range(2):
        for up in (True, False):
            for t in range(1, 9 if up == (part == 0) else 8):
                ring_copy(up, t, part).wait_send()


def local(wave, corr, kinetic, zslots, sticks, xlines, pot):
    plane, lines, forward, back = tables()
    dma = pltpu.SemaphoreType.DMA
    vmem = pltpu.VMEM
    return pl.pallas_call(
        kernel,
        out_shape=(
            jax.ShapeDtypeStruct((2, 1, K, SL), F32),
            jax.ShapeDtypeStruct((2, 1, NB), F32),
        ),
        in_specs=[pl.BlockSpec(memory_space=pltpu.HBM)] * 11,
        out_specs=(pl.BlockSpec(memory_space=vmem),) * 2,
        scratch_shapes=[
            vmem((2, 1, K, SL), F32),
            vmem((K, SL), F32),
            vmem((K, SL), jnp.int32),
            vmem((2, NF * SL), jnp.int32),
            vmem((1, L), jnp.int32),
            vmem((8, G * G), F32),
            vmem(plane.shape, BF16),
            vmem(lines.shape, BF16),
            vmem(forward.shape, BF16),
            vmem(back.shape, BF16),
            dma((11,)),
            vmem((NF, CPP, SL), F32),
            vmem((NF, CPP, SL), F32),
            vmem((NF, CPP, SL), F32),
            vmem((NF, CPP, SL), F32),
            vmem((2 * G, SL), F32),
            vmem((NB, 2, K, SL), F32),
            vmem((3, 4 * G, SL), F32),
            vmem((NC, GP, CS), BF16),
            vmem((NC, 1, CS), jnp.int32),
            vmem((2, CP * A, 2 * CS), BF16),
            vmem((2, CP * A, SL), F32),
            vmem((2, 3 * GP, 3 * GP), BF16),
            vmem((2 * G, 3 * GP), BF16),
            vmem((2 * L, 6 * G), BF16),
            vmem((2, 2 * L, 3 * GP), F32),
            vmem((2, CP * A, SL), F32),
            vmem((CP * A, 2 * GP), BF16),
            vmem((2 * G, SL), F32),
            vmem((NF, 1, SL), F32),
            vmem((NB, 1, SL), F32),
            dma((NF,)),
            dma((NF,)),
            dma((NF,)),
            dma((NF,)),
            dma((8, 2)),
            dma((8, 2)),
            dma((8, 2)),
            dma((8, 2)),
            dma((NF,)),
            dma((NF,)),
            dma((NB,)),
            dma((NB,)),
        ],
        compiler_params=pltpu.CompilerParams(
            collective_id=0,
            has_side_effects=True,
            vmem_limit_bytes=48 * 1024 * 1024,
        ),
    )(
        wave,
        corr,
        kinetic,
        zslots,
        sticks,
        xlines.reshape(1, L),
        pot,
        jnp.asarray(plane),
        jnp.asarray(lines),
        jnp.asarray(forward),
        jnp.asarray(back),
    )


def solution(mesh):
    return jax.shard_map(
        local,
        mesh=mesh,
        in_specs=(
            P(None, "band", None, "fft"),
            P(None, "band", None, "fft"),
            P(None, "fft"),
            P(None, "fft"),
            P(),
            P(),
            P("fft", None),
        ),
        out_specs=(P(None, "band", None, "fft"), P(None, "band", None)),
        check_vma=False,
    )
```
